256 devices in a mesh: sec: 2 (over y_hi), tile: 128 (over z, x, y_lo, core).
Axes of the slice: x: 4, y: 4 (y_hi: 2, y_lo: 2; y = y_hi * 2 + y_lo), z: 8, core: 2. Of those that a mesh axis runs over, the one named last changes fastest.
Arguments:
- atm_fields: bfloat16 [128, 1048576], P(None, ('sec', 'tile')), may hold values from -6 to 6
- remap_blocks: bfloat16 [16384, 4, 128, 128], P(('sec', 'tile')), may hold values from -0.25 to 0.25
- block_cols: int32 [16384, 4], P(('sec', 'tile')), may hold values from 0 to 8191, as said below
- flux_coef: float32 [32], replicated, may hold values from -1 to 1
- ocean_temp: float32 [1024, 2048], P(('sec', 'tile')), may hold values from -6 to 6
- sea_mask: int32 [1024, 2048], P(('sec', 'tile')), may hold values 0 or 1
Outputs:
- ocean_fields: bfloat16 [128, 2097152], P(None, ('sec', 'tile'))
- final_temp: float32 [1024, 2048], P(('sec', 'tile'))
The draws below stay inside these ranges and needn't reach their ends.
Inputs may be any that keep to these rules, and one draw needn't show every extreme that they name: `block_cols`: counting devices over sec+tile in order, an ocean tile of device d names only atmosphere tiles of devices d - 1, d and d + 1, that is tiles (32 (d - 1)) to (32 (d + 2) - 1).
All inputs are finite; a program needn't handle non-finite values. No bound on the sum of `sea_mask` on one device may be relied on, other than what follows from the above.
Results may differ from the reference program's by a relative error of at most 0.006.
Values may be sent and summed in bfloat16 or wider, within the bound.
A program may use at most 64 MiB of HBM per device.

```python
import jax
import jax.numpy as jnp
from jax import lax

F = 32
SUB = 4
K = 4
OX = 2048
ROWS = 128
OSTEPS = 2
OT_DEV = 64
AT_DEV = 32
NYO = 1024
OCEAN_TILES = 16384
ATM_TILES = 8192
N_SEC = 2
N_TILE = 128


def draw_block_cols(key, part):
    key = jax.random.fold_in(key, 11)
    owner = jnp.arange(OCEAN_TILES, dtype=jnp.int32) // OT_DEV
    offsets = jax.random.randint(key, (OCEAN_TILES, K), 0, 3 * AT_DEV, dtype=jnp.int32)
    columns = (owner[:, None] - 1) * AT_DEV + offsets
    columns = jnp.where(columns < 0, columns + AT_DEV, columns)
    columns = jnp.where(columns >= ATM_TILES, columns - AT_DEV, columns)
    return columns.astype(jnp.int32)


def plant(entries, stream_key, low, largest):
    shape = entries.shape
    index_at = [jax.random.randint(jax.random.fold_in(stream_key, axis), (), 0, shape[axis]) for axis in range(len(shape))]
    entries = entries.at[tuple(index_at)].set(low)
    longest = shape.index(max(shape))
    index_at[longest] = (index_at[longest] + 1) % shape[longest]
    return entries.at[tuple(index_at)].set(largest)


def level_of(key, extent, shards, least, top_value):
    factor_of = 1.0
    for position, parts in shards:
        steps = jax.random.uniform(jax.random.fold_in(jax.random.fold_in(key, 6), position), (parts,), jnp.float32, least / len(shards), top_value / len(shards))
        factor_of = factor_of * jnp.repeat(jnp.exp(steps), extent[position] // parts).reshape((-1,) + (1,) * (len(extent) - 1 - position))
    return factor_of


def gaussian(stream_key, shape, scale, most, split=(), held_as=jnp.bfloat16):
    array = jax.random.normal(stream_key, shape, jnp.float32) * scale
    if len(split) > 0:
        array = level_of(stream_key, shape, split, -0.22, 0.18) * array
    return jnp.clip(array, min=-most, max=most).astype(held_as)


def setup_inputs(seed: int = 0) -> dict:
    keys = jax.random.split(jax.random.key(seed), 7)
    atm_fields = gaussian(keys[0], (ROWS, ATM_TILES * 128), 1.0, 6.0, ((1, 256),))
    remap_blocks = gaussian(keys[1], (OCEAN_TILES, K, 128, 128), (K * 128) ** -0.5, 0.25, ((0, 256),))
    block_cols = draw_block_cols(jax.random.fold_in(keys[6], 71), 0)
    flux_coef = gaussian(keys[3], (F,), F ** -0.5, 1.0, (), jnp.float32)
    ocean_temp = gaussian(keys[4], (NYO, OX), 1.0, 6.0, ((0, 256),), jnp.float32)
    sea_mask = plant((jax.random.randint(keys[5], (NYO, OX), 0, 4) < 3).astype(jnp.int32), jax.random.fold_in(keys[5], 1), 0, 1)
    return dict(atm_fields=atm_fields, remap_blocks=remap_blocks, block_cols=block_cols, flux_coef=flux_coef, ocean_temp=ocean_temp, sea_mask=sea_mask)


DIFFUSE = 0.24
TIMESTEP = 0.5
RESTORE = 0.5


def sweep(padded, mask_pad, forcing, air_temp):
    centre = padded[1:-1]
    mask_mid = mask_pad[1:-1]

    def facing(other, other_mask):
        return other_mask * other + (1.0 - other_mask) * centre

    north = facing(padded[2:], mask_pad[2:])
    south = facing(padded[:-2], mask_pad[:-2])
    east = facing(jnp.roll(centre, -1, 1), jnp.roll(mask_mid, -1, 1))
    west = facing(jnp.roll(centre, 1, 1), jnp.roll(mask_mid, 1, 1))
    lap = north + south + east + west - 4.0 * centre
    return centre + mask_mid * (DIFFUSE * lap + TIMESTEP * forcing - TIMESTEP * RESTORE * (centre - air_temp))


def reference(atm_fields, remap_blocks, block_cols, flux_coef, ocean_temp, sea_mask):
    rows_n = atm_fields.shape[0]
    devices = N_SEC * N_TILE
    atm_tiles = atm_fields.reshape(rows_n, ATM_TILES, 128).transpose(1, 0, 2)
    blocks = remap_blocks.reshape(devices, OT_DEV, K, 128, 128)
    columns = block_cols.reshape(devices, OT_DEV, K)

    def one_band(operands):
        weights, cols = operands
        picked = jnp.take(atm_tiles, cols.reshape(-1).astype(jnp.int32), axis=0)
        picked = picked.reshape(OT_DEV, K, rows_n, 128)
        return jnp.einsum("tkrc,tkco->tro", picked.astype(jnp.float32), weights.astype(jnp.float32))

    remapped = lax.map(one_band, (blocks, columns))
    remapped = remapped.transpose(2, 0, 1, 3).reshape(rows_n, OCEAN_TILES * 128)
    ocean_fields = remapped.astype(jnp.bfloat16)
    fields = remapped.reshape(SUB, F, NYO, OX)
    net_heat = jnp.einsum("f,jfyx->jyx", flux_coef, fields, precision=lax.Precision.HIGHEST)
    forcing = 0.5 * (net_heat[0::2] + net_heat[1::2])
    air_temp = 0.5 * (fields[0::2, 0] + fields[1::2, 0])
    sea = sea_mask.astype(jnp.float32)
    mask_pad = jnp.pad(sea, ((1, 1), (0, 0)))
    temp = ocean_temp
    for step in range(OSTEPS):
        padded = jnp.pad(temp, ((1, 1), (0, 0)))
        temp = sweep(padded, mask_pad, forcing[step], air_temp[step])
    return ocean_fields, temp
```

```python
import functools

import jax
import jax.numpy as jnp
from jax import lax
from jax.experimental import pallas as pl
from jax.experimental.pallas import tpu as pltpu
from jax.sharding import PartitionSpec as P

MESH = pl.DeviceIdType.MESH
DIFFUSE = 0.24
TIMESTEP = 0.5
RESTORE = 0.5
CHUNKS = (32, 32, 32, 16, 16)
STARTS = tuple(sum(CHUNKS[:j]) for j in range(len(CHUNKS)))
EARLY = len(CHUNKS) - 1
HALF = 2
WEIGHT_PARTS = 4
LANES = 128


def fill_coef(coef, flux_ref):
    for f in range(coef.shape[0]):
        coef[f : f + 1, :] = jnp.full((1, LANES), 0.5 * flux_ref[f], jnp.float32)


def remap_rows(rows, first, across, bands, cols_ref, window, weights, coef, store, forcing, air):
    slots = cols_ref.shape[0]

    def column(xt, carry):
        heat, warm = [], []
        for y in range(bands):
            t = y * across + xt
            picked = jnp.concatenate(
                [
                    window[:, pl.ds(cols_ref[k, t] * LANES, LANES)]
                    for k in range(slots)
                ],
                axis=1,
            )
            total = jnp.dot(picked, weights[t], preferred_element_type=jnp.float32)
            store(t, total.astype(jnp.bfloat16))
            heat.append(jnp.sum(total * coef[first : first + rows, :], axis=0, keepdims=True))
            if first == 0:
                warm.append(0.5 * total[0:1, :])
        lanes = pl.ds(pl.multiple_of(xt * LANES, LANES), LANES)
        top = jnp.zeros((1, LANES), jnp.float32)
        low = jnp.zeros((8 - 1 - bands, LANES), jnp.float32)
        forcing[:, lanes] += jnp.concatenate([top] + heat + [low], axis=0)
        if first == 0:
            air[:, lanes] += jnp.concatenate([top] + warm + [low], axis=0)
        return carry

    lax.fori_loop(0, across, column, 0, unroll=across)


def sweep(centre, sea, masks, forcing, air):
    columns_n = centre.shape[1]
    lap = (
        masks[0] * (pltpu.roll(centre, 7, 0) - centre)
        + masks[1] * (pltpu.roll(centre, 1, 0) - centre)
        + masks[2] * (pltpu.roll(centre, columns_n - 1, 1) - centre)
        + masks[3] * (pltpu.roll(centre, 1, 1) - centre)
    )
    return centre + sea * (
        DIFFUSE * lap + TIMESTEP * forcing - TIMESTEP * RESTORE * (centre - air)
    )


def exchange_kernel(
    secs, tiles, fields_n, cols_hbm, flux_hbm, atm_ref, blocks_ref, temp_hbm, sea_hbm,
    weights, ocean, last, temp, sea, masks, forcing1, air1, coef, cols_ref,
    named_ref, flux_ref, temp_ref, sea_ref, windows, forcing0, air0,
    edge_out, edge_in, edge2_out, edge2_in,
    small_sem, own_sem, weight_sem, bulk_send, bulk_recv, edge_send, edge_recv, turn_sem,
):
    count = secs * tiles
    me = lax.axis_index("sec") * tiles + lax.axis_index("tile")
    right, left = lax.rem(me + 1, count), lax.rem(me + count - 1, count)

    def place(device):
        return (device // tiles, lax.rem(device, tiles))

    width = atm_ref.shape[1]
    ocean_count = cols_hbm.shape[1]
    bands, columns_n = temp_ref.shape
    across = columns_n // LANES
    sides = (right, left)
    there = (me < count - 1, me > 0)
    slabs = list(windows) + [last]

    def own_copy(j):
        return pltpu.make_async_copy(
            atm_ref.at[pl.ds(STARTS[j], CHUNKS[j])],
            slabs[j].at[:, pl.ds(width, width)],
            own_sem.at[j],
        )

    def weight_copy(p):
        part = ocean_count // WEIGHT_PARTS
        return pltpu.make_async_copy(
            blocks_ref.at[pl.ds(p * part, part)],
            weights.at[pl.ds(p * part, part)],
            weight_sem.at[p],
        )

    def bulk_copy(j, side):
        return pltpu.make_async_remote_copy(
            src_ref=atm_ref.at[pl.ds(STARTS[j], CHUNKS[j])],
            dst_ref=slabs[j].at[:, pl.ds(2 * width * side, width)],
            send_sem=bulk_send.at[side, j],
            recv_sem=bulk_recv.at[side, j],
            device_id=place(sides[side]),
            device_id_type=MESH,
        )

    def edge_copy(step, side):
        source, target = ((edge_out, edge_in), (edge2_out, edge2_in))[step]
        return pltpu.make_async_remote_copy(
            src_ref=source.at[side],
            dst_ref=target.at[side],
            send_sem=edge_send.at[step, side],
            recv_sem=edge_recv.at[step, side],
            device_id=place(sides[1 - side]),
            device_id_type=MESH,
        )

    odd = lax.rem(me, 2) == 1
    def held(device):
        tile = lax.rem(device, tiles)
        return ((lax.rem(tile, 4) == 0) & (tile > 0)) | ((lax.rem(tile, 4) == 3) & (tile < tiles - 1))

    waits = held(me)
    partner = me + 1 - 2 * lax.rem(me, 2)
    outward = (there[0] & odd, there[1] & ~odd)
    inward = (there[0] & ~odd, there[1] & odd)

    def send_off(j):
        for side in range(2):
            pl.when(outward[side])(bulk_copy(j, side).start)

    def send(j, late=True):
        if late:
            send_off(j)
        for side in range(2):
            pl.when(inward[side])(bulk_copy(j, side).start)

    barrier = pltpu.get_barrier_semaphore()
    for side in range(2):

        @pl.when(there[side])
        def _():
            pl.semaphore_signal(barrier, inc=1, device_id=place(sides[side]), device_id_type=MESH)

    smalls = [
        pltpu.make_async_copy(source, target, small_sem.at[i])
        for i, (source, target) in enumerate(
            ((temp_hbm, temp_ref), (sea_hbm, sea_ref), (cols_hbm, named_ref), (flux_hbm, flux_ref))
        )
    ]
    for copy in smalls:
        copy.start()
    pl.semaphore_wait(barrier, jnp.where((me == 0) | (me == count - 1), 1, 2))
    send(0)
    for j in range(len(CHUNKS)):
        own_copy(j).start()
    for copy in smalls:
        copy.wait()
    land = sea_ref[...].astype(jnp.float32)
    edge_out[0, 0:1, :] = temp_ref[0:1, :]
    edge_out[0, 1:2, :] = land[0:1, :]
    edge_out[1, 0:1, :] = temp_ref[bands - 1 : bands, :]
    edge_out[1, 1:2, :] = land[bands - 1 : bands, :]
    for side in range(2):
        pl.when(there[1 - side])(edge_copy(0, side).start)
    for j in range(1, HALF):
        send(j)
    for p in range(WEIGHT_PARTS):
        weight_copy(p).start()
    for j in range(HALF, len(CHUNKS)):
        send(j, late=False)
    pl.when(~waits)(lambda: send_off(HALF))
    temp[...] = jnp.zeros_like(temp)
    sea[...] = jnp.zeros_like(sea)
    temp[1 : 1 + bands, :] = temp_ref[...]
    sea[1 : 1 + bands, :] = land
    fill_coef(coef, flux_ref)
    for total in (forcing0, forcing1, air0, air1):
        total[...] = jnp.zeros_like(total)

    base = (me - 1) * (width // LANES)

    def locate(t, carry):
        for k in range(cols_ref.shape[0]):
            cols_ref[k, t] = jnp.clip(named_ref[k, t] - base, 0, 3 * (width // LANES) - 1)
        return carry

    lax.fori_loop(0, ocean_count, locate, 0, unroll=4)

    def first_sweep():
        for side in range(2):
            pl.when(there[side])(edge_copy(0, side).wait_recv)
        temp[0:1, :] = jnp.where(there[1], edge_in[1, 0:1, :], 0.0)
        temp[1 + bands : 2 + bands, :] = jnp.where(there[0], edge_in[0, 0:1, :], 0.0)
        sea[0:1, :] = jnp.where(there[1], edge_in[1, 1:2, :], 0.0)
        sea[1 + bands : 2 + bands, :] = jnp.where(there[0], edge_in[0, 1:2, :], 0.0)
        land = sea[...]
        masks[0] = pltpu.roll(land, 7, 0)
        masks[1] = pltpu.roll(land, 1, 0)
        masks[2] = pltpu.roll(land, columns_n - 1, 1)
        masks[3] = pltpu.roll(land, 1, 1)
        new = sweep(temp[...], sea[...], masks, forcing0[...], air0[...])
        edge2_out[0] = new[1:2, :]
        edge2_out[1] = new[bands : 1 + bands, :]
        for side in range(2):
            pl.when(there[1 - side])(edge_copy(1, side).start)
        temp[...] = new

    for p in range(WEIGHT_PARTS):
        weight_copy(p).wait()
    for j in range(EARLY):
        own_copy(j).wait()
        for side in range(2):
            pl.when(there[1 - side])(bulk_copy(j, side).wait_recv)
        if j == HALF - 1:

            @pl.when(held(partner))
            def _():
                pl.semaphore_signal(turn_sem, inc=1, device_id=place(partner), device_id_type=MESH)

        def store(t, value):
            ocean[STARTS[j] : STARTS[j] + CHUNKS[j], pl.ds(pl.multiple_of(t * LANES, LANES), LANES)] = value

        early = STARTS[j] < 2 * fields_n
        remap_rows(
            CHUNKS[j], STARTS[j] % fields_n, across, bands, cols_ref, slabs[j], weights, coef,
            store, forcing0 if early else forcing1, air0 if early else air1,
        )
        if STARTS[j] + CHUNKS[j] == 2 * fields_n:
            first_sweep()

            @pl.when(waits)
            def _():
                pl.semaphore_wait(turn_sem, 1)
                send_off(HALF)

            for later in range(HALF + 1, len(CHUNKS)):
                send_off(later)

    for side in range(2):
        pl.when(there[side])(edge_copy(1, side).wait_recv)
    temp[0:1, :] = jnp.where(there[1], edge2_in[1], 0.0)
    temp[1 + bands : 2 + bands, :] = jnp.where(there[0], edge2_in[0], 0.0)
    for step in range(2):
        for side in range(2):
            pl.when(there[1 - side])(edge_copy(step, side).wait_send)
    own_copy(EARLY).wait()
    for j in range(len(CHUNKS)):
        for side in range(2):
            pl.when(there[side])(bulk_copy(j, side).wait_send)
    for side in range(2):
        pl.when(there[1 - side])(bulk_copy(EARLY, side).wait_recv)


def finish_kernel(
    fields_n, cols_ref, weights, ocean, last, temp, sea, masks, forcing_in, air, coef,
    out_ref, final_ref,
    forcing, late, final, sems,
):
    bands, columns_n = final.shape
    across = columns_n // LANES
    early = pltpu.make_async_copy(ocean, out_ref.at[pl.ds(0, STARTS[EARLY])], sems.at[0])
    early.start()
    forcing[...] = forcing_in[...]

    def store(t, value):
        late[:, pl.ds(pl.multiple_of(t * LANES, LANES), LANES)] = value

    remap_rows(
        CHUNKS[EARLY], STARTS[EARLY] % fields_n, across, bands, cols_ref, last, weights, coef,
        store, forcing, None,
    )
    rest = pltpu.make_async_copy(late, out_ref.at[pl.ds(STARTS[EARLY], CHUNKS[EARLY])], sems.at[1])
    rest.start()
    final[...] = sweep(temp[...], sea[...], masks, forcing[...], air[...])[1 : 1 + bands, :]
    done = pltpu.make_async_copy(final, final_ref, sems.at[2])
    done.start()
    early.wait()
    rest.wait()
    done.wait()


def solution(mesh):
    secs, tiles = mesh.shape["sec"], mesh.shape["tile"]

    def body(atm_fields, remap_blocks, block_cols, flux_coef, ocean_temp, sea_mask):
        rows_n, width = atm_fields.shape
        ocean_count, slots = block_cols.shape
        bands, columns_n = ocean_temp.shape
        fields_n = flux_coef.shape[0]
        chunks = len(CHUNKS)
        blocks = remap_blocks.reshape(ocean_count, slots * LANES, LANES)
        vmem = pl.BlockSpec(memory_space=pltpu.VMEM)
        smem = pl.BlockSpec(memory_space=pltpu.SMEM)
        hbm = pl.BlockSpec(memory_space=pltpu.HBM)
        grid_state = (8, columns_n)
        inputs = [
            pltpu.with_memory_space_constraint(x, pltpu.HBM)
            for x in (block_cols.T, flux_coef, atm_fields, blocks, ocean_temp, sea_mask)
        ]
        state = pl.pallas_call(
            functools.partial(exchange_kernel, secs, tiles, fields_n),
            out_shape=(
                pltpu.VMEM(blocks.shape, jnp.bfloat16),
                pltpu.VMEM((STARTS[EARLY], ocean_count * LANES), jnp.bfloat16),
                pltpu.VMEM((CHUNKS[EARLY], 3 * width), jnp.bfloat16),
                pltpu.VMEM(grid_state, jnp.float32),
                pltpu.VMEM(grid_state, jnp.float32),
                pltpu.VMEM((4,) + grid_state, jnp.float32),
                pltpu.VMEM(grid_state, jnp.float32),
                pltpu.VMEM(grid_state, jnp.float32),
                pltpu.VMEM((fields_n, LANES), jnp.float32),
                pltpu.SMEM((slots, ocean_count), jnp.int32),
            ),
            in_specs=[hbm] * 6,
            out_specs=[vmem] * 9 + [smem],
            scratch_shapes=[
                pltpu.SMEM((slots, ocean_count), jnp.int32),
                pltpu.SMEM((fields_n,), jnp.float32),
                pltpu.VMEM((bands, columns_n), jnp.float32),
                pltpu.VMEM((bands, columns_n), jnp.int32),
                [pltpu.VMEM((r, 3 * width), jnp.bfloat16) for r in CHUNKS[:EARLY]],
                pltpu.VMEM(grid_state, jnp.float32),
                pltpu.VMEM(grid_state, jnp.float32),
                pltpu.VMEM((2, 2, columns_n), jnp.float32),
                pltpu.VMEM((2, 2, columns_n), jnp.float32),
                pltpu.VMEM((2, 1, columns_n), jnp.float32),
                pltpu.VMEM((2, 1, columns_n), jnp.float32),
                pltpu.SemaphoreType.DMA((4,)),
                pltpu.SemaphoreType.DMA((chunks,)),
                pltpu.SemaphoreType.DMA((WEIGHT_PARTS,)),
                pltpu.SemaphoreType.DMA((2, chunks)),
                pltpu.SemaphoreType.DMA((2, chunks)),
                pltpu.SemaphoreType.DMA((2, 2)),
                pltpu.SemaphoreType.DMA((2, 2)),
                pltpu.SemaphoreType.REGULAR,
            ],
            compiler_params=pltpu.CompilerParams(
                collective_id=0, has_side_effects=True, vmem_limit_bytes=16 << 20
            ),
            name="exchange",
        )(*inputs)
        weights, ocean, last, temp, sea, masks, forcing, air, coef, cols = state
        kept = [
            pltpu.with_memory_space_constraint(x, pltpu.VMEM)
            for x in (weights, ocean, last, temp, sea, masks, forcing, air, coef)
        ]
        return pl.pallas_call(
            functools.partial(finish_kernel, fields_n),
            out_shape=(
                pltpu.HBM((rows_n, ocean_count * LANES), jnp.bfloat16),
                pltpu.HBM((bands, columns_n), jnp.float32),
            ),
            in_specs=[smem] + [vmem] * 9,
            out_specs=(hbm, hbm),
            scratch_shapes=[
                pltpu.VMEM(grid_state, jnp.float32),
                pltpu.VMEM((CHUNKS[EARLY], ocean_count * LANES), jnp.bfloat16),
                pltpu.VMEM((bands, columns_n), jnp.float32),
                pltpu.SemaphoreType.DMA((3,)),
            ],
            compiler_params=pltpu.CompilerParams(vmem_limit_bytes=8 << 20),
            name="finish",
        )(pltpu.with_memory_space_constraint(cols, pltpu.SMEM), *kept)

    band = P(("sec", "tile"), None)
    return jax.shard_map(
        body,
        mesh=mesh,
        in_specs=(P(None, ("sec", "tile")), P(("sec", "tile"), None, None, None), band, P(), band, band),
        out_specs=(P(None, ("sec", "tile")), band),
        check_vma=False,
    )
```

```python
import functools

import jax
import jax.numpy as jnp
from jax import lax
from jax.experimental import pallas as pl
from jax.experimental.pallas import tpu as pltpu
from jax.sharding import PartitionSpec as P

MESH = pl.DeviceIdType.MESH
DIFFUSE = 0.24
TIMESTEP = 0.5
RESTORE = 0.5
CHUNKS = (32, 32, 32, 16, 16)
STARTS = tuple(sum(CHUNKS[:j]) for j in range(len(CHUNKS)))
EARLY = len(CHUNKS) - 1
HALF = 2
WEIGHT_PARTS = 4
LANES = 128


def fill_coef(coef, flux_ref):
    for f in range(coef.shape[0]):
        coef[f : f + 1, :] = jnp.full((1, LANES), 0.5 * flux_ref[f], jnp.float32)


def remap_rows(rows, first, band, cols_ref, window, weights, coef, store, add):
    slots = cols_ref.shape[0]
    bands, columns_n = band
    across = columns_n // LANES

    def column(xt, carry):
        heat, warm = [], []
        for y in range(bands):
            t = y * across + xt
            picked = jnp.concatenate(
                [window[:, pl.ds(cols_ref[k, t] * LANES, LANES)] for k in range(slots)], axis=1
            )
            total = jnp.dot(picked, weights[t], preferred_element_type=jnp.float32)
            store(t, total.astype(jnp.bfloat16))
            heat.append(jnp.sum(total * coef[first : first + rows, :], axis=0, keepdims=True))
            warm.append(0.5 * total[0:1, :])
        add(
            pl.ds(pl.multiple_of(xt * LANES, LANES), LANES),
            jnp.concatenate(heat, axis=0),
            jnp.concatenate(warm, axis=0) if first == 0 else None,
        )
        return carry

    lax.fori_loop(0, across, column, 0, unroll=across)


def sweep(centre, sea, masks, forcing, air):
    columns_n = centre.shape[1]
    lap = (
        masks[0] * (pltpu.roll(centre, 7, 0) - centre)
        + masks[1] * (pltpu.roll(centre, 1, 0) - centre)
        + masks[2] * (pltpu.roll(centre, columns_n - 1, 1) - centre)
        + masks[3] * (pltpu.roll(centre, 1, 1) - centre)
    )
    return centre + sea * (
        DIFFUSE * lap + TIMESTEP * forcing - TIMESTEP * RESTORE * (centre - air)
    )


def exchange_kernel(
    secs, tiles, fields_n, cols_hbm, flux_hbm, atm_ref, blocks_ref, temp_hbm, sea_hbm,
    weights, ocean, last, base, sea_out, coef, cols_ref,
    named_ref, flux_ref, temp_ref, sea_ref, windows, temp, sea, masks, forcing0, air0, forcing1, air1,
    edge_out, edge_in, edge2_out, edge2_in,
    small_sem, own_sem, weight_sem, bulk_send, bulk_recv, edge_send, edge_recv, turn_sem,
):
    count = secs * tiles
    me = lax.axis_index("sec") * tiles + lax.axis_index("tile")
    right, left = lax.rem(me + 1, count), lax.rem(me + count - 1, count)

    def place(device):
        return (device // tiles, lax.rem(device, tiles))

    width = atm_ref.shape[1]
    ocean_count = cols_hbm.shape[1]
    bands, columns_n = temp_ref.shape
    across = columns_n // LANES
    sides = (right, left)
    there = (me < count - 1, me > 0)
    slabs = list(windows) + [last]

    def own_copy(j):
        return pltpu.make_async_copy(
            atm_ref.at[pl.ds(STARTS[j], CHUNKS[j])],
            slabs[j].at[:, pl.ds(width, width)],
            own_sem.at[j],
        )

    def weight_copy(p):
        part = ocean_count // WEIGHT_PARTS
        return pltpu.make_async_copy(
            blocks_ref.at[pl.ds(p * part, part)],
            weights.at[pl.ds(p * part, part)],
            weight_sem.at[p],
        )

    def bulk_copy(j, side):
        return pltpu.make_async_remote_copy(
            src_ref=atm_ref.at[pl.ds(STARTS[j], CHUNKS[j])],
            dst_ref=slabs[j].at[:, pl.ds(2 * width * side, width)],
            send_sem=bulk_send.at[side, j],
            recv_sem=bulk_recv.at[side, j],
            device_id=place(sides[side]),
            device_id_type=MESH,
        )

    def edge_copy(step, side):
        source, target = ((edge_out, edge_in), (edge2_out, edge2_in))[step]
        return pltpu.make_async_remote_copy(
            src_ref=source.at[side],
            dst_ref=target.at[side],
            send_sem=edge_send.at[step, side],
            recv_sem=edge_recv.at[step, side],
            device_id=place(sides[1 - side]),
            device_id_type=MESH,
        )

    odd = lax.rem(me, 2) == 1
    def held(device):
        tile = lax.rem(device, tiles)
        return ((lax.rem(tile, 4) == 0) & (tile > 0)) | ((lax.rem(tile, 4) == 3) & (tile < tiles - 1))

    waits = held(me)
    partner = me + 1 - 2 * lax.rem(me, 2)
    outward = (there[0] & odd, there[1] & ~odd)
    inward = (there[0] & ~odd, there[1] & odd)

    def send_off(j):
        for side in range(2):
            pl.when(outward[side])(bulk_copy(j, side).start)

    def send(j, late=True):
        if late:
            send_off(j)
        for side in range(2):
            pl.when(inward[side])(bulk_copy(j, side).start)

    barrier = pltpu.get_barrier_semaphore()
    for side in range(2):

        @pl.when(there[side])
        def _():
            pl.semaphore_signal(barrier, inc=1, device_id=place(sides[side]), device_id_type=MESH)

    smalls = [
        pltpu.make_async_copy(source, target, small_sem.at[i])
        for i, (source, target) in enumerate(
            ((temp_hbm, temp_ref), (sea_hbm, sea_ref), (cols_hbm, named_ref), (flux_hbm, flux_ref))
        )
    ]
    for copy in smalls:
        copy.start()
    pl.semaphore_wait(barrier, jnp.where((me == 0) | (me == count - 1), 1, 2))
    send(0)
    for j in range(len(CHUNKS)):
        own_copy(j).start()
    for copy in smalls:
        copy.wait()
    land = sea_ref[...].astype(jnp.float32)
    edge_out[0, 0:1, :] = temp_ref[0:1, :]
    edge_out[0, 1:2, :] = land[0:1, :]
    edge_out[1, 0:1, :] = temp_ref[bands - 1 : bands, :]
    edge_out[1, 1:2, :] = land[bands - 1 : bands, :]
    for side in range(2):
        pl.when(there[1 - side])(edge_copy(0, side).start)
    for j in range(1, HALF):
        send(j)
    for p in range(WEIGHT_PARTS):
        weight_copy(p).start()
    for j in range(HALF, len(CHUNKS)):
        send(j, late=False)
    pl.when(~waits)(lambda: send_off(HALF))
    pl.when(~waits)(lambda: send_off(HALF + 1))
    temp[...] = jnp.zeros_like(temp)
    sea[...] = jnp.zeros_like(sea)
    temp[1 : 1 + bands, :] = temp_ref[...]
    sea[1 : 1 + bands, :] = land
    fill_coef(coef, flux_ref)
    for total in (forcing0, forcing1, air0, air1):
        total[...] = jnp.zeros_like(total)

    lowest = (me - 1) * (width // LANES)

    def locate(t, carry):
        for k in range(cols_ref.shape[0]):
            cols_ref[k, t] = jnp.clip(named_ref[k, t] - lowest, 0, 3 * (width // LANES) - 1)
        return carry

    lax.fori_loop(0, ocean_count, locate, 0, unroll=4)

    def first_sweep():
        for side in range(2):
            pl.when(there[side])(edge_copy(0, side).wait_recv)
        temp[0:1, :] = jnp.where(there[1], edge_in[1, 0:1, :], 0.0)
        temp[1 + bands : 2 + bands, :] = jnp.where(there[0], edge_in[0, 0:1, :], 0.0)
        sea[0:1, :] = jnp.where(there[1], edge_in[1, 1:2, :], 0.0)
        sea[1 + bands : 2 + bands, :] = jnp.where(there[0], edge_in[0, 1:2, :], 0.0)
        land = sea[...]
        masks[0] = pltpu.roll(land, 7, 0)
        masks[1] = pltpu.roll(land, 1, 0)
        masks[2] = pltpu.roll(land, columns_n - 1, 1)
        masks[3] = pltpu.roll(land, 1, 1)
        new = sweep(temp[...], sea[...], masks, forcing0[...], air0[...])
        edge2_out[0] = new[1:2, :]
        edge2_out[1] = new[bands : 1 + bands, :]
        for side in range(2):
            pl.when(there[1 - side])(edge_copy(1, side).start)
        temp[...] = new

    for p in range(WEIGHT_PARTS):
        weight_copy(p).wait()
    for j in range(EARLY):
        own_copy(j).wait()
        for side in range(2):
            pl.when(there[1 - side])(bulk_copy(j, side).wait_recv)
        if j == HALF - 1:

            @pl.when(held(partner))
            def _():
                pl.semaphore_signal(turn_sem, inc=1, device_id=place(partner), device_id_type=MESH)

        def store(t, value):
            ocean[STARTS[j] : STARTS[j] + CHUNKS[j], pl.ds(pl.multiple_of(t * LANES, LANES), LANES)] = value

        early = STARTS[j] < 2 * fields_n
        forcing, air = (forcing0, air0) if early else (forcing1, air1)

        def add(lanes, heat, warm):
            forcing[1 : 1 + bands, lanes] += heat
            if warm is not None:
                air[1 : 1 + bands, lanes] += warm

        remap_rows(
            CHUNKS[j], STARTS[j] % fields_n, (bands, columns_n), cols_ref, slabs[j], weights, coef, store, add
        )
        if STARTS[j] + CHUNKS[j] == 2 * fields_n:
            first_sweep()

            @pl.when(waits)
            def _():
                pl.semaphore_wait(turn_sem, 1)
                send_off(HALF)
                send_off(HALF + 1)

            for later in range(HALF + 2, len(CHUNKS)):
                send_off(later)

    for side in range(2):
        pl.when(there[side])(edge_copy(1, side).wait_recv)
    temp[0:1, :] = jnp.where(there[1], edge2_in[1], 0.0)
    temp[1 + bands : 2 + bands, :] = jnp.where(there[0], edge2_in[0], 0.0)
    base[...] = sweep(temp[...], sea[...], masks, forcing1[...], air1[...])[1 : 1 + bands, :]
    sea_out[...] = sea_ref[...].astype(jnp.float32)
    for step in range(2):
        for side in range(2):
            pl.when(there[1 - side])(edge_copy(step, side).wait_send)
    own_copy(EARLY).wait()
    for j in range(len(CHUNKS)):
        for side in range(2):
            pl.when(there[side])(bulk_copy(j, side).wait_send)
    for side in range(2):
        pl.when(there[1 - side])(bulk_copy(EARLY, side).wait_recv)


def finish_kernel(
    fields_n, cols_ref, weights, ocean, last, base, sea, coef, out_ref, final_ref, late, final, sems
):
    step = CHUNKS[EARLY]

    def early(i):
        rows = pl.ds(pl.multiple_of(i * step, step), step)
        return pltpu.make_async_copy(ocean.at[rows], out_ref.at[rows], sems.at[2 + i])

    lax.fori_loop(0, STARTS[EARLY] // step, lambda i, carry: (early(i).start(), carry)[1], 0)

    def store(t, value):
        late[:, pl.ds(pl.multiple_of(t * LANES, LANES), LANES)] = value

    def add(lanes, heat, warm):
        final[:, lanes] = base[:, lanes] + sea[:, lanes] * (TIMESTEP * heat)

    remap_rows(
        CHUNKS[EARLY], STARTS[EARLY] % fields_n, final.shape, cols_ref, last, weights, coef, store, add
    )
    rest = pltpu.make_async_copy(late, out_ref.at[pl.ds(STARTS[EARLY], step)], sems.at[0])
    rest.start()
    done = pltpu.make_async_copy(final, final_ref, sems.at[1])
    done.start()
    lax.fori_loop(0, STARTS[EARLY] // step, lambda i, carry: (early(i).wait(), carry)[1], 0)
    rest.wait()
    done.wait()


def solution(mesh):
    secs, tiles = mesh.shape["sec"], mesh.shape["tile"]

    def body(atm_fields, remap_blocks, block_cols, flux_coef, ocean_temp, sea_mask):
        rows_n, width = atm_fields.shape
        ocean_count, slots = block_cols.shape
        bands, columns_n = ocean_temp.shape
        fields_n = flux_coef.shape[0]
        chunks = len(CHUNKS)
        blocks = remap_blocks.reshape(ocean_count, slots * LANES, LANES)
        vmem = pl.BlockSpec(memory_space=pltpu.VMEM)
        smem = pl.BlockSpec(memory_space=pltpu.SMEM)
        hbm = pl.BlockSpec(memory_space=pltpu.HBM)
        grid_state = (8, columns_n)
        inputs = [
            pltpu.with_memory_space_constraint(x, pltpu.HBM)
            for x in (block_cols.T, flux_coef, atm_fields, blocks, ocean_temp, sea_mask)
        ]
        state = pl.pallas_call(
            functools.partial(exchange_kernel, secs, tiles, fields_n),
            out_shape=(
                pltpu.VMEM(blocks.shape, jnp.bfloat16),
                pltpu.VMEM((STARTS[EARLY], ocean_count * LANES), jnp.bfloat16),
                pltpu.VMEM((CHUNKS[EARLY], 3 * width), jnp.bfloat16),
                pltpu.VMEM((bands, columns_n), jnp.float32),
                pltpu.VMEM((bands, columns_n), jnp.float32),
                pltpu.VMEM((fields_n, LANES), jnp.float32),
                pltpu.SMEM((slots, ocean_count), jnp.int32),
            ),
            in_specs=[hbm] * 6,
            out_specs=[vmem] * 6 + [smem],
            scratch_shapes=[
                pltpu.SMEM((slots, ocean_count), jnp.int32),
                pltpu.SMEM((fields_n,), jnp.float32),
                pltpu.VMEM((bands, columns_n), jnp.float32),
                pltpu.VMEM((bands, columns_n), jnp.int32),
                [pltpu.VMEM((r, 3 * width), jnp.bfloat16) for r in CHUNKS[:EARLY]],
                pltpu.VMEM(grid_state, jnp.float32),
                pltpu.VMEM(grid_state, jnp.float32),
                pltpu.VMEM((4,) + grid_state, jnp.float32),
                pltpu.VMEM(grid_state, jnp.float32),
                pltpu.VMEM(grid_state, jnp.float32),
                pltpu.VMEM(grid_state, jnp.float32),
                pltpu.VMEM(grid_state, jnp.float32),
                pltpu.VMEM((2, 2, columns_n), jnp.float32),
                pltpu.VMEM((2, 2, columns_n), jnp.float32),
                pltpu.VMEM((2, 1, columns_n), jnp.float32),
                pltpu.VMEM((2, 1, columns_n), jnp.float32),
                pltpu.SemaphoreType.DMA((4,)),
                pltpu.SemaphoreType.DMA((chunks,)),
                pltpu.SemaphoreType.DMA((WEIGHT_PARTS,)),
                pltpu.SemaphoreType.DMA((2, chunks)),
                pltpu.SemaphoreType.DMA((2, chunks)),
                pltpu.SemaphoreType.DMA((2, 2)),
                pltpu.SemaphoreType.DMA((2, 2)),
                pltpu.SemaphoreType.REGULAR,
            ],
            compiler_params=pltpu.CompilerParams(
                collective_id=0, has_side_effects=True, vmem_limit_bytes=16 << 20
            ),
            name="exchange",
        )(*inputs)
        kept = [pltpu.with_memory_space_constraint(x, pltpu.VMEM) for x in state[:-1]]
        return pl.pallas_call(
            functools.partial(finish_kernel, fields_n),
            out_shape=(
                pltpu.HBM((rows_n, ocean_count * LANES), jnp.bfloat16),
                pltpu.HBM((bands, columns_n), jnp.float32),
            ),
            in_specs=[smem] + [vmem] * 6,
            out_specs=(hbm, hbm),
            scratch_shapes=[
                pltpu.VMEM((CHUNKS[EARLY], ocean_count * LANES), jnp.bfloat16),
                pltpu.VMEM((bands, columns_n), jnp.float32),
                pltpu.SemaphoreType.DMA((2 + STARTS[EARLY] // CHUNKS[EARLY],)),
            ],
            compiler_params=pltpu.CompilerParams(vmem_limit_bytes=8 << 20),
            name="finish",
        )(pltpu.with_memory_space_constraint(state[-1], pltpu.SMEM), *kept)

    band = P(("sec", "tile"), None)
    return jax.shard_map(
        body,
        mesh=mesh,
        in_specs=(P(None, ("sec", "tile")), P(("sec", "tile"), None, None, None), band, P(), band, band),
        out_specs=(P(None, ("sec", "tile")), band),
        check_vma=False,
    )
```

```python
import functools

import jax
import jax.numpy as jnp
from jax import lax
from jax.experimental import pallas as pl
from jax.experimental.pallas import tpu as pltpu
from jax.sharding import PartitionSpec as P

MESH = pl.DeviceIdType.MESH
DIFFUSE = 0.24
TIMESTEP = 0.5
RESTORE = 0.5
CHUNKS = (32, 32, 32, 16, 16)
STARTS = tuple(sum(CHUNKS[:j]) for j in range(len(CHUNKS)))
EARLY = len(CHUNKS) - 1
HALF = 2
WEIGHT_PARTS = 4
LANES = 128


def fill_coef(coef, flux_ref):
    for f in range(coef.shape[0]):
        coef[f : f + 1, :] = jnp.full((1, LANES), 0.5 * flux_ref[f], jnp.float32)


def remap_rows(rows, first, band, cols_ref, window, weights, coef, store, add):
    slots = cols_ref.shape[0]
    bands, columns_n = band
    across = columns_n // LANES

    def column(xt, carry):
        heat, warm = [], []
        for y in range(bands):
            t = y * across + xt
            picked = jnp.concatenate(
                [window[:, pl.ds(cols_ref[k, t] * LANES, LANES)] for k in range(slots)], axis=1
            )
            total = jnp.dot(picked, weights[t], preferred_element_type=jnp.float32)
            store(t, total.astype(jnp.bfloat16))
            heat.append(jnp.sum(total * coef[first : first + rows, :], axis=0, keepdims=True))
            warm.append(0.5 * total[0:1, :])
        add(
            pl.ds(pl.multiple_of(xt * LANES, LANES), LANES),
            jnp.concatenate(heat, axis=0),
            jnp.concatenate(warm, axis=0) if first == 0 else None,
        )
        return carry

    lax.fori_loop(0, across, column, 0, unroll=across)


def sweep(centre, sea, masks, forcing, air):
    columns_n = centre.shape[1]
    lap = (
        masks[0] * (pltpu.roll(centre, 7, 0) - centre)
        + masks[1] * (pltpu.roll(centre, 1, 0) - centre)
        + masks[2] * (pltpu.roll(centre, columns_n - 1, 1) - centre)
        + masks[3] * (pltpu.roll(centre, 1, 1) - centre)
    )
    return centre + sea * (
        DIFFUSE * lap + TIMESTEP * forcing - TIMESTEP * RESTORE * (centre - air)
    )


def exchange_kernel(
    secs, tiles, fields_n, cols_hbm, flux_hbm, atm_ref, blocks_ref, temp_hbm, sea_hbm,
    weights, ocean, last, base, sea_out, coef, cols_ref,
    named_ref, flux_ref, temp_ref, sea_ref, windows, temp, sea, masks, forcing0, air0, forcing1, air1,
    edge_out, edge_in, edge2_out, edge2_in,
    small_sem, own_sem, weight_sem, bulk_send, bulk_recv, edge_send, edge_recv, turn_sem,
):
    count = secs * tiles
    me = lax.axis_index("sec") * tiles + lax.axis_index("tile")
    right, left = lax.rem(me + 1, count), lax.rem(me + count - 1, count)

    def place(device):
        return (device // tiles, lax.rem(device, tiles))

    width = atm_ref.shape[1]
    ocean_count = cols_hbm.shape[1]
    bands, columns_n = temp_ref.shape
    across = columns_n // LANES
    sides = (right, left)
    there = (me < count - 1, me > 0)
    slabs = list(windows) + [last]

    def own_copy(j):
        return pltpu.make_async_copy(
            atm_ref.at[pl.ds(STARTS[j], CHUNKS[j])],
            slabs[j].at[:, pl.ds(width, width)],
            own_sem.at[j],
        )

    def weight_copy(p):
        part = ocean_count // WEIGHT_PARTS
        return pltpu.make_async_copy(
            blocks_ref.at[pl.ds(p * part, part)],
            weights.at[pl.ds(p * part, part)],
            weight_sem.at[p],
        )

    def bulk_copy(j, side):
        return pltpu.make_async_remote_copy(
            src_ref=atm_ref.at[pl.ds(STARTS[j], CHUNKS[j])],
            dst_ref=slabs[j].at[:, pl.ds(2 * width * side, width)],
            send_sem=bulk_send.at[side, j],
            recv_sem=bulk_recv.at[side, j],
            device_id=place(sides[side]),
            device_id_type=MESH,
        )

    def edge_copy(step, side):
        source, target = ((edge_out, edge_in), (edge2_out, edge2_in))[step]
        return pltpu.make_async_remote_copy(
            src_ref=source.at[side],
            dst_ref=target.at[side],
            send_sem=edge_send.at[step, side],
            recv_sem=edge_recv.at[step, side],
            device_id=place(sides[1 - side]),
            device_id_type=MESH,
        )

    odd = lax.rem(me, 2) == 1
    def held(device):
        tile = lax.rem(device, tiles)
        return ((lax.rem(tile, 4) == 0) & (lax.rem(tile, 16) > 0)) | ((lax.rem(tile, 4) == 3) & (lax.rem(tile, 16) < 15))

    waits = held(me)
    partner = me + 1 - 2 * lax.rem(me, 2)
    eager = ~waits & ~held(partner)
    outward = (there[0] & odd, there[1] & ~odd)
    inward = (there[0] & ~odd, there[1] & odd)

    def send_off(j):
        for side in range(2):
            pl.when(outward[side])(bulk_copy(j, side).start)

    def send(j, late=True):
        if late:
            send_off(j)
        for side in range(2):
            pl.when(inward[side])(bulk_copy(j, side).start)

    barrier = pltpu.get_barrier_semaphore()
    for side in range(2):

        @pl.when(there[side])
        def _():
            pl.semaphore_signal(barrier, inc=1, device_id=place(sides[side]), device_id_type=MESH)

    smalls = [
        pltpu.make_async_copy(source, target, small_sem.at[i])
        for i, (source, target) in enumerate(
            ((temp_hbm, temp_ref), (sea_hbm, sea_ref), (cols_hbm, named_ref), (flux_hbm, flux_ref))
        )
    ]
    for copy in smalls:
        copy.start()
    pl.semaphore_wait(barrier, jnp.where((me == 0) | (me == count - 1), 1, 2))
    send(0)
    for j in range(len(CHUNKS)):
        own_copy(j).start()
    for copy in smalls:
        copy.wait()
    land = sea_ref[...].astype(jnp.float32)
    edge_out[0, 0:1, :] = temp_ref[0:1, :]
    edge_out[0, 1:2, :] = land[0:1, :]
    edge_out[1, 0:1, :] = temp_ref[bands - 1 : bands, :]
    edge_out[1, 1:2, :] = land[bands - 1 : bands, :]
    for side in range(2):
        pl.when(there[1 - side])(edge_copy(0, side).start)
    for j in range(1, HALF):
        send(j)
    for p in range(WEIGHT_PARTS):
        weight_copy(p).start()
    for j in range(HALF, len(CHUNKS)):
        send(j, late=False)
    pl.when(~waits)(lambda: send_off(HALF))
    pl.when(~waits)(lambda: send_off(HALF + 1))
    pl.when(eager)(lambda: send_off(EARLY))
    temp[...] = jnp.zeros_like(temp)
    sea[...] = jnp.zeros_like(sea)
    temp[1 : 1 + bands, :] = temp_ref[...]
    sea[1 : 1 + bands, :] = land
    fill_coef(coef, flux_ref)
    for total in (forcing0, forcing1, air0, air1):
        total[...] = jnp.zeros_like(total)

    lowest = (me - 1) * (width // LANES)

    def locate(t, carry):
        for k in range(cols_ref.shape[0]):
            cols_ref[k, t] = jnp.clip(named_ref[k, t] - lowest, 0, 3 * (width // LANES) - 1)
        return carry

    lax.fori_loop(0, ocean_count, locate, 0, unroll=4)

    def first_sweep():
        for side in range(2):
            pl.when(there[side])(edge_copy(0, side).wait_recv)
        temp[0:1, :] = jnp.where(there[1], edge_in[1, 0:1, :], 0.0)
        temp[1 + bands : 2 + bands, :] = jnp.where(there[0], edge_in[0, 0:1, :], 0.0)
        sea[0:1, :] = jnp.where(there[1], edge_in[1, 1:2, :], 0.0)
        sea[1 + bands : 2 + bands, :] = jnp.where(there[0], edge_in[0, 1:2, :], 0.0)
        land = sea[...]
        masks[0] = pltpu.roll(land, 7, 0)
        masks[1] = pltpu.roll(land, 1, 0)
        masks[2] = pltpu.roll(land, columns_n - 1, 1)
        masks[3] = pltpu.roll(land, 1, 1)
        new = sweep(temp[...], sea[...], masks, forcing0[...], air0[...])
        edge2_out[0] = new[1:2, :]
        edge2_out[1] = new[bands : 1 + bands, :]
        for side in range(2):
            pl.when(there[1 - side])(edge_copy(1, side).start)
        temp[...] = new

    for p in range(WEIGHT_PARTS):
        weight_copy(p).wait()
    for j in range(EARLY):
        own_copy(j).wait()
        for side in range(2):
            pl.when(there[1 - side])(bulk_copy(j, side).wait_recv)
        if j == HALF - 1:

            @pl.when(held(partner))
            def _():
                pl.semaphore_signal(turn_sem, inc=1, device_id=place(partner), device_id_type=MESH)

        def store(t, value):
            ocean[STARTS[j] : STARTS[j] + CHUNKS[j], pl.ds(pl.multiple_of(t * LANES, LANES), LANES)] = value

        early = STARTS[j] < 2 * fields_n
        forcing, air = (forcing0, air0) if early else (forcing1, air1)

        def add(lanes, heat, warm):
            forcing[1 : 1 + bands, lanes] += heat
            if warm is not None:
                air[1 : 1 + bands, lanes] += warm

        remap_rows(
            CHUNKS[j], STARTS[j] % fields_n, (bands, columns_n), cols_ref, slabs[j], weights, coef, store, add
        )
        if STARTS[j] + CHUNKS[j] == 2 * fields_n:
            first_sweep()

            @pl.when(waits)
            def _():
                pl.semaphore_wait(turn_sem, 1)
                send_off(HALF)
                send_off(HALF + 1)

            pl.when(~eager)(lambda: send_off(EARLY))

    for side in range(2):
        pl.when(there[side])(edge_copy(1, side).wait_recv)
    temp[0:1, :] = jnp.where(there[1], edge2_in[1], 0.0)
    temp[1 + bands : 2 + bands, :] = jnp.where(there[0], edge2_in[0], 0.0)
    base[...] = sweep(temp[...], sea[...], masks, forcing1[...], air1[...])[1 : 1 + bands, :]
    sea_out[...] = sea_ref[...].astype(jnp.float32)
    for step in range(2):
        for side in range(2):
            pl.when(there[1 - side])(edge_copy(step, side).wait_send)
    own_copy(EARLY).wait()
    for j in range(len(CHUNKS)):
        for side in range(2):
            pl.when(there[side])(bulk_copy(j, side).wait_send)
    for side in range(2):
        pl.when(there[1 - side])(bulk_copy(EARLY, side).wait_recv)


def finish_kernel(
    fields_n, cols_ref, weights, ocean, last, base, sea, coef, out_ref, final_ref, late, final, sems
):
    step = CHUNKS[EARLY]

    def early(i):
        rows = pl.ds(pl.multiple_of(i * step, step), step)
        return pltpu.make_async_copy(ocean.at[rows], out_ref.at[rows], sems.at[2 + i])

    lax.fori_loop(0, STARTS[EARLY] // step, lambda i, carry: (early(i).start(), carry)[1], 0)

    def store(t, value):
        late[:, pl.ds(pl.multiple_of(t * LANES, LANES), LANES)] = value

    def add(lanes, heat, warm):
        final[:, lanes] = base[:, lanes] + sea[:, lanes] * (TIMESTEP * heat)

    remap_rows(
        CHUNKS[EARLY], STARTS[EARLY] % fields_n, final.shape, cols_ref, last, weights, coef, store, add
    )
    rest = pltpu.make_async_copy(late, out_ref.at[pl.ds(STARTS[EARLY], step)], sems.at[0])
    rest.start()
    done = pltpu.make_async_copy(final, final_ref, sems.at[1])
    done.start()
    lax.fori_loop(0, STARTS[EARLY] // step, lambda i, carry: (early(i).wait(), carry)[1], 0)
    rest.wait()
    done.wait()


def solution(mesh):
    secs, tiles = mesh.shape["sec"], mesh.shape["tile"]

    def body(atm_fields, remap_blocks, block_cols, flux_coef, ocean_temp, sea_mask):
        rows_n, width = atm_fields.shape
        ocean_count, slots = block_cols.shape
        bands, columns_n = ocean_temp.shape
        fields_n = flux_coef.shape[0]
        chunks = len(CHUNKS)
        blocks = remap_blocks.reshape(ocean_count, slots * LANES, LANES)
        vmem = pl.BlockSpec(memory_space=pltpu.VMEM)
        smem = pl.BlockSpec(memory_space=pltpu.SMEM)
        hbm = pl.BlockSpec(memory_space=pltpu.HBM)
        grid_state = (8, columns_n)
        inputs = [
            pltpu.with_memory_space_constraint(x, pltpu.HBM)
            for x in (block_cols.T, flux_coef, atm_fields, blocks, ocean_temp, sea_mask)
        ]
        state = pl.pallas_call(
            functools.partial(exchange_kernel, secs, tiles, fields_n),
            out_shape=(
                pltpu.VMEM(blocks.shape, jnp.bfloat16),
                pltpu.VMEM((STARTS[EARLY], ocean_count * LANES), jnp.bfloat16),
                pltpu.VMEM((CHUNKS[EARLY], 3 * width), jnp.bfloat16),
                pltpu.VMEM((bands, columns_n), jnp.float32),
                pltpu.VMEM((bands, columns_n), jnp.float32),
                pltpu.VMEM((fields_n, LANES), jnp.float32),
                pltpu.SMEM((slots, ocean_count), jnp.int32),
            ),
            in_specs=[hbm] * 6,
            out_specs=[vmem] * 6 + [smem],
            scratch_shapes=[
                pltpu.SMEM((slots, ocean_count), jnp.int32),
                pltpu.SMEM((fields_n,), jnp.float32),
                pltpu.VMEM((bands, columns_n), jnp.float32),
                pltpu.VMEM((bands, columns_n), jnp.int32),
                [pltpu.VMEM((r, 3 * width), jnp.bfloat16) for r in CHUNKS[:EARLY]],
                pltpu.VMEM(grid_state, jnp.float32),
                pltpu.VMEM(grid_state, jnp.float32),
                pltpu.VMEM((4,) + grid_state, jnp.float32),
                pltpu.VMEM(grid_state, jnp.float32),
                pltpu.VMEM(grid_state, jnp.float32),
                pltpu.VMEM(grid_state, jnp.float32),
                pltpu.VMEM(grid_state, jnp.float32),
                pltpu.VMEM((2, 2, columns_n), jnp.float32),
                pltpu.VMEM((2, 2, columns_n), jnp.float32),
                pltpu.VMEM((2, 1, columns_n), jnp.float32),
                pltpu.VMEM((2, 1, columns_n), jnp.float32),
                pltpu.SemaphoreType.DMA((4,)),
                pltpu.SemaphoreType.DMA((chunks,)),
                pltpu.SemaphoreType.DMA((WEIGHT_PARTS,)),
                pltpu.SemaphoreType.DMA((2, chunks)),
                pltpu.SemaphoreType.DMA((2, chunks)),
                pltpu.SemaphoreType.DMA((2, 2)),
                pltpu.SemaphoreType.DMA((2, 2)),
                pltpu.SemaphoreType.REGULAR,
            ],
            compiler_params=pltpu.CompilerParams(
                collective_id=0, has_side_effects=True, vmem_limit_bytes=16 << 20
            ),
            name="exchange",
        )(*inputs)
        kept = [pltpu.with_memory_space_constraint(x, pltpu.VMEM) for x in state[:-1]]
        return pl.pallas_call(
            functools.partial(finish_kernel, fields_n),
            out_shape=(
                pltpu.HBM((rows_n, ocean_count * LANES), jnp.bfloat16),
                pltpu.HBM((bands, columns_n), jnp.float32),
            ),
            in_specs=[smem] + [vmem] * 6,
            out_specs=(hbm, hbm),
            scratch_shapes=[
                pltpu.VMEM((CHUNKS[EARLY], ocean_count * LANES), jnp.bfloat16),
                pltpu.VMEM((bands, columns_n), jnp.float32),
                pltpu.SemaphoreType.DMA((2 + STARTS[EARLY] // CHUNKS[EARLY],)),
            ],
            compiler_params=pltpu.CompilerParams(vmem_limit_bytes=8 << 20),
            name="finish",
        )(pltpu.with_memory_space_constraint(state[-1], pltpu.SMEM), *kept)

    band = P(("sec", "tile"), None)
    return jax.shard_map(
        body,
        mesh=mesh,
        in_specs=(P(None, ("sec", "tile")), P(("sec", "tile"), None, None, None), band, P(), band, band),
        out_specs=(P(None, ("sec", "tile")), band),
        check_vma=False,
    )
```
